32 devices in a mesh: pipe: 4 (over y, x), expert: 8 (over z, core).
Axes of the slice: x: 2, y: 2, z: 4, core: 2. Of those that a mesh axis runs over, the one named last changes fastest.
Arguments:
- grad_rows: bfloat16 [2, 4, 1024, 3584], P(None, 'pipe', 'expert'), may hold values from -0.29882812 to 0.29882812
- expert_ids: int32 [2, 4, 1024, 8], P(None, 'pipe', 'expert'), may hold values from 0 to 7, all different within a row; in each aligned block of 128 rows (0 to 127, 128 to 255, ..., all dimensions but the last counted through in order) at most 128 rows name the same one
- gate_buckets: int32 [2, 4, 1024, 8], P(None, 'pipe', 'expert'), may hold values from 1 to 64
- saved_hidden: bfloat16 [2, 4, 8, 1024, 1280], P(None, 'pipe', 'expert'), may hold values from -6 to 6
Outputs:
- weight_grad: bfloat16 [4, 8, 1280, 3584], P('pipe', 'expert')
The draws below stay inside these ranges and needn't reach their ends.
Inputs may be any that keep to these rules, and one draw needn't show every extreme that they name: `expert_ids`: in every direction and rank, each aligned block of 128 tokens names each expert in at most 128 routes and some expert in exactly 128; the 8 ids of a token differ.
All inputs are finite; a program needn't handle non-finite values.
Results may differ from the reference program's by a relative error of at most 0.0058.
Values may be sent and summed in bfloat16 or wider, within the bound.
No kernel may reach another device: no remote copies, remote signals or barrier semaphores. Data moves between devices by JAX's collectives and lax.ppermute only.
A program may use at most 128 MiB of HBM per device.

```python
import math
import jax
import jax.numpy as jnp
import numpy as np
from jax import lax

D = 3584
F = 1280
TOPK = 8
TOK_DEV = 128
EXPERTS = 8
TOKENS = 1024
CAP = 128
SLOTS = 1024
N_PIPE = 4
N_EXPERT = 8


def with_ends(drawn, key, least, largest):
    dims = drawn.shape
    spot = [jax.random.randint(jax.random.fold_in(key, axis), (), 0, dims[axis]) for axis in range(len(dims))]
    drawn = drawn.at[tuple(spot)].set(least)
    longest = dims.index(max(dims))
    spot[longest] = (spot[longest] + 1) % dims[longest]
    return drawn.at[tuple(spot)].set(largest)


def shard_levels(own_key, shape, cuts, smallest, top_value):
    loudness = 1.0
    for dim, blocks in cuts:
        heights = jax.random.uniform(jax.random.fold_in(jax.random.fold_in(own_key, 6), dim), (blocks,), jnp.float32, smallest / len(cuts), top_value / len(cuts))
        loudness = loudness * jnp.repeat(jnp.exp(heights), shape[dim] // blocks).reshape((-1,) + (1,) * (len(shape) - 1 - dim))
    return loudness


def assign_block(rng, own, number, rows, count, top, most, skew):
    ranking = jax.random.permutation(rng, count)
    packed, common = load_shares(count, rows * top, most, skew, True), load_shares(count, rows * top, most, skew, False)
    places = jnp.arange(count)

    def named(lengths, offset_by):
        used = int((lengths > 0).sum())
        fixed = max(1, used // 4)
        shifted = fixed + (places - fixed + offset_by * (used - fixed)) % max(1, count - fixed)
        return jnp.zeros((count,), jnp.int32).at[ranking[jnp.where(places < fixed, places, shifted)]].set(jnp.asarray(lengths, jnp.int32))

    lengths = jnp.where(number % 4 == 0, named(packed, number // 4), named(common, number - number // 4 - 1))
    mixed = jax.random.permutation(jax.random.fold_in(own, 3), count)
    donor, sink = mixed[0:count // 2 * 2:2], mixed[1:count // 2 * 2:2]
    margin = jnp.minimum(lengths[donor] - 1, most - lengths[sink]) // 2
    margin = jnp.where((donor == ranking[0]) | (sink == ranking[0]) | (lengths[sink] == 0), 0, jnp.maximum(margin, 0))
    shifted = jax.random.randint(jax.random.fold_in(own, 4), (count // 2,), 0, 1 << 20) % (margin + 1)
    lengths = lengths.at[donor].add(-shifted).at[sink].add(shifted)
    items = jnp.searchsorted(jnp.cumsum(lengths), jnp.arange(rows * top), side="right").astype(jnp.int32)
    grid = items.reshape(top, rows).T
    grid = grid[jax.random.permutation(jax.random.fold_in(own, 1), rows)]
    offset_by = jax.random.randint(jax.random.fold_in(own, 2), (rows, 1), 0, top)
    return jnp.take_along_axis(grid, (jnp.arange(top)[None, :] + offset_by) % top, axis=1)


def load_shares(number_of, total, reach, slope, full):
    loads = [(1 << 20) // math.isqrt(grade ** slope) + 1 for grade in range(1, number_of + 1)]
    largest = reach if full else min(reach, max(-(-total // number_of), total * loads[0] // sum(loads)))
    least = 1 if total - largest >= number_of - 1 else 0
    given, surplus = [largest] + [least] * (number_of - 1), total - largest - least * (number_of - 1)
    while surplus > 0:
        movable = [i for i in range(1, number_of) if given[i] < largest] or [i for i in range(1, number_of) if given[i] < reach]
        pool, left = sum([loads[i] for i in movable]), surplus
        for i in movable:
            extra = min(reach - given[i], max(1, left * loads[i] // pool), surplus)
            given[i] = given[i] + extra
            surplus = surplus - extra
    return np.array(given)


def noise(rng, dims, scale, reach, split=(), kind=jnp.bfloat16):
    drawn = jax.random.normal(rng, dims, jnp.float32) * scale
    if len(split) > 0:
        drawn = shard_levels(rng, dims, split, -0.22, 0.18) * drawn
    return jnp.clip(drawn, min=-reach, max=reach).astype(kind)


def setup_inputs(seed: int = 0) -> dict:
    keys = jax.random.split(jax.random.key(seed), 5)
    grad_rows = noise(keys[0], (2, N_PIPE, TOKENS, D), 0.05, 0.29882812, ((1, 4), (2, 8)))
    expert_ids_keys = jax.random.split(jax.random.fold_in(keys[1], 1), 2 * N_PIPE * TOKENS // TOK_DEV)
    expert_ids_turns = jax.random.permutation(jax.random.fold_in(keys[1], 3), 2 * N_PIPE * TOKENS // TOK_DEV)
    expert_ids = jax.vmap(lambda own, number: assign_block(jax.random.fold_in(keys[1], 2), own, number, TOK_DEV, EXPERTS, TOPK, CAP, 1))(expert_ids_keys, expert_ids_turns).reshape((2, N_PIPE, TOKENS, TOPK))
    gate_buckets = with_ends(jax.random.randint(keys[2], (2, N_PIPE, TOKENS, TOPK), 1, 65), jax.random.fold_in(keys[2], 1), 1, 64).astype(jnp.int32)
    saved_hidden = noise(keys[3], (2, N_PIPE, EXPERTS, SLOTS, F), 1.0, 6.0, ((1, 4), (2, 8)))
    return {"grad_rows": grad_rows, "expert_ids": expert_ids, "gate_buckets": gate_buckets, "saved_hidden": saved_hidden}


def build_outbound(token_rows, route_ids, bucket_ids):
    flat_ids = route_ids.reshape(-1)
    one_hot = (flat_ids[:, None] == jnp.arange(EXPERTS, dtype=jnp.int32)[None, :]).astype(jnp.int32)
    earlier = jnp.cumsum(one_hot, axis=0) - one_hot
    position = jnp.sum(earlier * one_hot, axis=1)
    slot_ids = flat_ids * CAP + position
    weighting = bucket_ids.reshape(-1).astype(jnp.float32) / 64.0
    slot_table = (slot_ids[:, None] == jnp.arange(EXPERTS * CAP, dtype=jnp.int32)[None, :]).astype(jnp.float32)
    slot_table = slot_table * weighting[:, None]
    spread = jnp.sum(slot_table.reshape(TOK_DEV, TOPK, EXPERTS * CAP), axis=1).astype(jnp.bfloat16)
    outbound = lax.dot_general(spread, token_rows, (((0,), (0,)), ((), ())), preferred_element_type=jnp.float32)
    return outbound.astype(jnp.bfloat16).reshape(EXPERTS, CAP, D)


def arrived_rows(token_rows, route_ids, bucket_ids):
    blocks = (token_rows.reshape(N_EXPERT, TOK_DEV, D), route_ids.reshape(N_EXPERT, TOK_DEV, TOPK), bucket_ids.reshape(N_EXPERT, TOK_DEV, TOPK))
    sent = lax.map(lambda pieces: build_outbound(pieces[0], pieces[1], pieces[2]), blocks)
    return jnp.moveaxis(sent, 1, 0).reshape(EXPERTS, SLOTS, D)


def per_expert(pieces):
    first_in, second_in, first_hidden, second_hidden = pieces
    first_part = jnp.dot(first_hidden.T, first_in, preferred_element_type=jnp.float32).astype(jnp.bfloat16)
    second_part = jnp.dot(second_hidden.T, second_in, preferred_element_type=jnp.float32).astype(jnp.bfloat16)
    return (first_part.astype(jnp.float32) + second_part.astype(jnp.float32)).astype(jnp.bfloat16)


def reference(grad_rows, expert_ids, gate_buckets, saved_hidden):
    section_grads = []
    for section in range(N_PIPE):
        mirror = N_PIPE - 1 - section
        first_in = arrived_rows(grad_rows[0, section], expert_ids[0, section], gate_buckets[0, section])
        second_in = arrived_rows(grad_rows[1, mirror], expert_ids[1, mirror], gate_buckets[1, mirror])
        section_grads.append(lax.map(per_expert, (first_in, second_in, saved_hidden[0, section], saved_hidden[1, mirror])))
    return jnp.stack(section_grads)
```

```python
import functools
import jax
import jax.numpy as jnp
from jax import lax
from jax.experimental import pallas as pl
from jax.experimental.pallas import tpu as pltpu
from jax.sharding import PartitionSpec as P

BF16 = jnp.bfloat16
F32 = jnp.float32
TILE = 256


def mirror(shard):
    ranks = lax.axis_size("pipe")
    return lax.ppermute(shard, "pipe", [(i, ranks - 1 - i) for i in range(ranks)])


def core_swap(shard):
    count = lax.axis_size("expert")
    return lax.ppermute(shard, "expert", [(i, i ^ 1) for i in range(count)])


def chip_shift(shard):
    count = lax.axis_size("expert")
    return lax.ppermute(shard, "expert", [(i, (i + 2) % count) for i in range(count)])


def after(value, *earlier):
    return lax.optimization_barrier((value,) + earlier)[0]


def build_outbound(token_rows, route_ids, bucket_ids, experts, capacity):
    tok_count, top_count = route_ids.shape
    flat_ids = route_ids.reshape(-1)
    one_hot = (flat_ids[:, None] == jnp.arange(experts, dtype=jnp.int32)[None, :]).astype(jnp.int32)
    earlier = jnp.cumsum(one_hot, axis=0) - one_hot
    position = jnp.sum(earlier * one_hot, axis=1)
    slot_ids = flat_ids * capacity + position
    weighting = bucket_ids.reshape(-1).astype(F32) / 64.0
    slot_table = (
        slot_ids[:, None] == jnp.arange(experts * capacity, dtype=jnp.int32)[None, :]
    ).astype(F32)
    slot_table = slot_table * weighting[:, None]
    spread = jnp.sum(slot_table.reshape(tok_count, top_count, experts * capacity), axis=1).astype(BF16)
    outbound = lax.dot_general(
        spread, token_rows, (((0,), (0,)), ((), ())), preferred_element_type=F32
    )
    return outbound.astype(BF16).reshape(experts, capacity, token_rows.shape[1])


def slot_product(hidden_rows, inbound):
    flat_in = inbound.reshape(-1, inbound.shape[-1])
    product = lax.dot_general(
        hidden_rows, flat_in, (((0,), (0,)), ((), ())), preferred_element_type=F32
    )
    return product.astype(BF16)


def routed(token_rows, route_ids, bucket_ids, hidden_rows, experts, capacity):
    partials = []
    for index in range(2):
        outbound = build_outbound(
            token_rows[index], route_ids[index], bucket_ids[index], experts, capacity
        )
        arrived = lax.all_to_all(outbound, "expert", split_axis=0, concat_axis=0, tiled=True)
        partials.append(slot_product(hidden_rows[index], arrived))
    return (partials[0].astype(F32) + mirror(partials[1]).astype(F32)).astype(BF16)


def scale_kernel(order_ref, hidden_ref, gate_ref, out_ref):
    turned = hidden_ref[...].astype(F32).T
    out_ref[...] = (turned * gate_ref[0]).astype(BF16)


def scaled_transposed(order, hidden, gates):
    blocks, _, rows = gates.shape
    width = hidden.shape[1]
    return pl.pallas_call(
        scale_kernel,
        grid_spec=pltpu.PrefetchScalarGridSpec(
            num_scalar_prefetch=1,
            grid=(blocks,),
            in_specs=[
                pl.BlockSpec((rows, width), lambda i, order: (order[i], 0)),
                pl.BlockSpec((1, 1, rows), lambda i, order: (order[i], 0, 0)),
            ],
            out_specs=pl.BlockSpec((width, rows), lambda i, order: (0, i)),
        ),
        out_shape=jax.ShapeDtypeStruct((width, blocks * rows), BF16),
        compiler_params=pltpu.CompilerParams(vmem_limit_bytes=16 << 20),
        cost_estimate=pl.CostEstimate(
            flops=hidden.size, bytes_accessed=4 * hidden.size, transcendentals=0
        ),
        name="scale_hidden",
    )(order, hidden, gates)


def product_kernel(count, add, hidden_ref, *refs):
    rows = jnp.concatenate([ref[...] for ref in refs[:count]], axis=0)
    product = jnp.dot(hidden_ref[...], rows, preferred_element_type=F32)
    if add:
        product = product + refs[count][...].astype(F32)
    refs[-1][...] = product.astype(BF16)


def block_product(hidden, pieces, total, column, width, add):
    out_rows, depth = hidden.shape
    chunk = pieces[0].shape[1]
    first = column // TILE
    in_specs = [pl.BlockSpec((out_rows, depth), lambda j: (0, 0))]
    in_specs += [pl.BlockSpec((p.shape[0], TILE), lambda j: (0, j)) for p in pieces]
    operands = [hidden, *pieces]
    aliases = {}
    out_spec = pl.BlockSpec((out_rows, TILE), lambda j: (0, first + j))
    if total is not None:
        in_specs.append(out_spec if add else pl.BlockSpec(memory_space=pl.ANY))
        aliases = {len(operands): 0}
        operands.append(total)
    return pl.pallas_call(
        functools.partial(product_kernel, len(pieces), add),
        grid=(chunk // TILE,),
        in_specs=in_specs,
        out_specs=out_spec,
        out_shape=jax.ShapeDtypeStruct((out_rows, width), BF16),
        input_output_aliases=aliases,
        compiler_params=pltpu.CompilerParams(vmem_limit_bytes=32 << 20),
        cost_estimate=pl.CostEstimate(
            flops=2 * out_rows * depth * chunk,
            bytes_accessed=2 * (out_rows * depth + depth * chunk + 2 * out_rows * chunk),
            transcendentals=0,
        ),
        name="block_product",
    )(*operands)


def gathered(token_rows, route_ids, bucket_ids, hidden_rows, experts):
    width = token_rows.shape[2]
    steps = experts // 2
    me = lax.axis_index("expert")
    rank = lax.axis_index("pipe")
    ranks = lax.axis_size("pipe")
    order = jnp.stack(
        [2 * lax.rem(me // 2 + steps - i // 2, steps) + (me % 2 ^ i % 2) for i in range(experts)]
    ).astype(jnp.int32)

    named = route_ids[:, None] == jnp.arange(experts, dtype=jnp.int32)[None, :, None, None]
    gates = jnp.sum(jnp.where(named, bucket_ids[:, None], 0), axis=3).astype(F32) / 64.0
    all_gates = lax.all_gather(gates, ("pipe", "expert"), axis=0, tiled=False)
    all_gates = all_gates.reshape((ranks, experts) + gates.shape)
    all_gates = lax.dynamic_index_in_dim(all_gates, me, axis=3, keepdims=True)
    gates_0 = lax.dynamic_index_in_dim(all_gates[:, :, 0], rank, axis=0, keepdims=False)
    gates_1 = lax.dynamic_index_in_dim(all_gates[:, :, 1], ranks - 1 - rank, axis=0, keepdims=False)

    cut = (width // 2) // TILE * TILE
    spans = [(0, cut), (cut, width)]
    rows_1 = mirror(token_rows[1])
    hidden_1 = mirror(hidden_rows[1])
    sent = []
    pieces = [[[] for _ in spans] for _ in range(2)]
    for direction, source in enumerate((token_rows[0], rows_1)):
        if direction == 1:
            source = after(source, sent[-3])
        held = [source[:, lo:hi] for lo, hi in spans]
        for step in range(steps):
            for index in range(len(spans)):
                block = held[index]
                pieces[direction][index] += [block, core_swap(block)]
                if step < steps - 1:
                    held[index] = chip_shift(block)
                    sent.append(held[index])

    scaled_0 = scaled_transposed(order, hidden_rows[0], gates_0)
    scaled_1 = scaled_transposed(order, hidden_1, gates_1)
    total = None
    for index, (lo, _) in enumerate(spans):
        total = block_product(scaled_0, pieces[0][index], total, lo, width, False)
    for index, (lo, _) in enumerate(spans):
        total = block_product(scaled_1, pieces[1][index], total, lo, width, True)
    return total


def on_device(grad_rows, expert_ids, gate_buckets, saved_hidden):
    experts = lax.axis_size("expert")
    capacity = saved_hidden.shape[3] // experts
    tok_count, top_count = expert_ids.shape[2:]
    token_rows, route_ids, bucket_ids = grad_rows[:, 0], expert_ids[:, 0], gate_buckets[:, 0]
    hidden_rows = saved_hidden[:, 0, 0]
    if top_count == experts and capacity == tok_count and experts % 2 == 0:
        result = gathered(token_rows, route_ids, bucket_ids, hidden_rows, experts)
    else:
        result = routed(token_rows, route_ids, bucket_ids, hidden_rows, experts, capacity)
    return result[None, None]


def solution(mesh):
    return jax.shard_map(
        on_device,
        mesh=mesh,
        in_specs=(
            P(None, "pipe", "expert", None),
            P(None, "pipe", "expert", None),
            P(None, "pipe", "expert", None),
            P(None, "pipe", "expert", None, None),
        ),
        out_specs=P("pipe", "expert", None, None),
        check_vma=False,
    )
```

```python
import functools
import jax
import jax.numpy as jnp
from jax import lax
from jax.experimental import pallas as pl
from jax.experimental.pallas import tpu as pltpu
from jax.sharding import PartitionSpec as P

BF16 = jnp.bfloat16
F32 = jnp.float32
LANES = 128
PARTS = 5
TOKEN = (16, 128)
VMEM_SMALL = 8 << 20
VMEM = 24 << 20
VMEM_PACK = 58 << 20
WITH_C = 2
HOLD_D = True
TOK_A = TOK_B = TOK_C = True
C_AFTER = 1
TM_P = 2
SUM = BF16
VMEM_SCALE = 8 << 20
VMEM_FIRST = 24 << 20
CUT = 0.5


def mirror(shard):
    ranks = lax.axis_size("pipe")
    return lax.ppermute(shard, "pipe", [(i, ranks - 1 - i) for i in range(ranks)])


def core_swap(shard):
    count = lax.axis_size("expert")
    return lax.ppermute(shard, "expert", [(i, i ^ 1) for i in range(count)])


def chip_shift(shard):
    count = lax.axis_size("expert")
    return lax.ppermute(shard, "expert", [(i, (i + 2) % count) for i in range(count)])


def build_outbound(token_rows, route_ids, bucket_ids, experts, capacity):
    tok_count, top_count = route_ids.shape
    flat_ids = route_ids.reshape(-1)
    one_hot = (flat_ids[:, None] == jnp.arange(experts, dtype=jnp.int32)[None, :]).astype(jnp.int32)
    earlier = jnp.cumsum(one_hot, axis=0) - one_hot
    position = jnp.sum(earlier * one_hot, axis=1)
    slot_ids = flat_ids * capacity + position
    weighting = bucket_ids.reshape(-1).astype(F32) / 64.0
    slot_table = (
        slot_ids[:, None] == jnp.arange(experts * capacity, dtype=jnp.int32)[None, :]
    ).astype(F32)
    slot_table = slot_table * weighting[:, None]
    spread = jnp.sum(slot_table.reshape(tok_count, top_count, experts * capacity), axis=1).astype(BF16)
    outbound = lax.dot_general(
        spread, token_rows, (((0,), (0,)), ((), ())), preferred_element_type=F32
    )
    return outbound.astype(BF16).reshape(experts, capacity, token_rows.shape[1])


def slot_product(hidden_rows, inbound):
    flat_in = inbound.reshape(-1, inbound.shape[-1])
    product = lax.dot_general(
        hidden_rows, flat_in, (((0,), (0,)), ((), ())), preferred_element_type=F32
    )
    return product.astype(BF16)


def routed(token_rows, route_ids, bucket_ids, hidden_rows, experts, capacity):
    partials = []
    for index in range(2):
        outbound = build_outbound(
            token_rows[index], route_ids[index], bucket_ids[index], experts, capacity
        )
        arrived = lax.all_to_all(outbound, "expert", split_axis=0, concat_axis=0, tiled=True)
        partials.append(slot_product(hidden_rows[index], arrived))
    return (partials[0].astype(F32) + mirror(partials[1]).astype(F32)).astype(BF16)


def moved(count):
    return pl.CostEstimate(flops=0, bytes_accessed=1024, transcendentals=0)


def pack_kernel(spans, has_gates, rows_ref, *refs):
    outs = refs[len(refs) - len(spans) - 1:-1]
    refs[-1][...] = jnp.zeros_like(refs[-1])
    for (lo, hi), out_ref in zip(spans, outs):
        for start in range(lo, hi, LANES):
            out_ref[start - lo:start - lo + LANES, :] = rows_ref[0, 0, :, start:start + LANES]
        if has_gates:
            out_ref[hi - lo:, :] = refs[0][...]


def pack(grad_rows, direction, spans, gates, *deps):
    tokens, width = grad_rows.shape[2:]
    extra = 0 if gates is None else gates.shape[0]
    shapes = [(hi - lo + extra, LANES) for lo, hi in spans]
    in_specs = [pl.BlockSpec((1, 1, tokens, width), lambda i: (direction, 0, 0, 0))]
    operands = [grad_rows]
    if gates is not None:
        in_specs.append(pl.BlockSpec(gates.shape, lambda i: (0, 0)))
        operands.append(gates)
    return pl.pallas_call(
        functools.partial(pack_kernel, spans, gates is not None),
        grid=(1,),
        in_specs=in_specs + [pl.BlockSpec(memory_space=pl.ANY)] * len(deps),
        out_specs=[pl.BlockSpec(shape, lambda i: (0, 0)) for shape in shapes + [TOKEN]],
        out_shape=[jax.ShapeDtypeStruct(shape, BF16) for shape in shapes + [TOKEN]],
        compiler_params=pltpu.CompilerParams(vmem_limit_bytes=VMEM_PACK),
        cost_estimate=moved(4 * tokens * width),
        name="pack_rows",
    )(*operands, *deps)


def pack_second_kernel(span, order_ref, rows_ref, *refs):
    *hidden_refs, _, out_ref, token_ref = refs
    lo, hi = span
    for start in range(lo, hi, LANES):
        out_ref[start - lo:start - lo + LANES, :] = rows_ref[0, 0, :, start:start + LANES]
    for i, ref in enumerate(hidden_refs):
        base = hi - lo + i * ref.shape[4]
        out_ref[base:base + ref.shape[4], :] = ref[0, 0, 0].T
    token_ref[...] = jnp.zeros_like(token_ref)


def pack_second(order, grad_rows, saved_hidden, span, blocks, dep):
    tokens, width = grad_rows.shape[2:]
    out_rows = saved_hidden.shape[4]
    shape = (span[1] - span[0] + len(blocks) * out_rows, LANES)

    def hidden_spec(i):
        return pl.BlockSpec((1, 1, 1, LANES, out_rows), lambda g, order: (1, 0, 0, order[i], 0))

    return pl.pallas_call(
        functools.partial(pack_second_kernel, span),
        grid_spec=pltpu.PrefetchScalarGridSpec(
            num_scalar_prefetch=1,
            grid=(1,),
            in_specs=[pl.BlockSpec((1, 1, tokens, width), lambda g, order: (1, 0, 0, 0))]
            + [hidden_spec(i) for i in blocks]
            + [pl.BlockSpec(memory_space=pl.ANY)],
            out_specs=[
                pl.BlockSpec(shape, lambda g, order: (0, 0)),
                pl.BlockSpec(TOKEN, lambda g, order: (0, 0)),
            ],
        ),
        out_shape=[jax.ShapeDtypeStruct(shape, BF16), jax.ShapeDtypeStruct(TOKEN, BF16)],
        compiler_params=pltpu.CompilerParams(vmem_limit_bytes=VMEM_PACK),
        cost_estimate=moved(1024),
        name="pack_second",
    )(order, grad_rows, *([saved_hidden] * len(blocks)), dep)


def top_kernel(in_ref, *refs):
    refs[-1][...] = in_ref[...]


def top(value, rows, *deps):
    spec = pl.BlockSpec((rows, LANES), lambda i: (0, 0))
    return pl.pallas_call(
        top_kernel,
        grid=(1,),
        in_specs=[spec] + [pl.BlockSpec(memory_space=pl.ANY)] * len(deps),
        out_specs=spec,
        out_shape=jax.ShapeDtypeStruct((rows, LANES), BF16),
        compiler_params=pltpu.CompilerParams(vmem_limit_bytes=VMEM_SMALL),
        cost_estimate=moved(1024),
        name="top_rows",
    )(value, *deps)


def hold_kernel(*refs):
    pass


def hold(value, *deps):
    return pl.pallas_call(
        hold_kernel,
        in_specs=[pl.BlockSpec(memory_space=pl.ANY)] * (1 + len(deps)),
        out_specs=pl.BlockSpec(memory_space=pl.ANY),
        out_shape=jax.ShapeDtypeStruct(value.shape, value.dtype),
        input_output_aliases={0: 0},
        compiler_params=pltpu.CompilerParams(vmem_limit_bytes=VMEM_SMALL),
        cost_estimate=moved(1024),
        name="hold",
    )(value, *deps)


def turn_kernel(hidden_ref, _, out_ref, token_ref):
    slots = hidden_ref.shape[3]
    for i in range(slots // LANES):
        lanes = slice(i * LANES, (i + 1) * LANES)
        out_ref[:, lanes] = hidden_ref[0, 0, 0, lanes, :].T
    token_ref[...] = jnp.zeros_like(token_ref)


def turned(saved_hidden, dep):
    slots, width = saved_hidden.shape[3:]
    return pl.pallas_call(
        turn_kernel,
        grid=(1,),
        in_specs=[
            pl.BlockSpec((1, 1, 1, slots, width), lambda i: (0, 0, 0, 0, 0)),
            pl.BlockSpec(memory_space=pl.ANY),
        ],
        out_specs=[
            pl.BlockSpec((width, slots), lambda i: (0, 0)),
            pl.BlockSpec(TOKEN, lambda i: (0, 0)),
        ],
        out_shape=[jax.ShapeDtypeStruct((width, slots), BF16), jax.ShapeDtypeStruct(TOKEN, BF16)],
        compiler_params=pltpu.CompilerParams(vmem_limit_bytes=VMEM_PACK),
        cost_estimate=moved(1024),
        name="turn_hidden",
    )(saved_hidden, dep)


def first_scale_kernel(rows_ref, hidden_ref, *refs):
    *packet_refs, out_ref, other_ref = refs
    index = lax.broadcasted_iota(jnp.int32, packet_refs[0].shape, 0)
    for i, ref in enumerate(packet_refs):
        lanes = slice(i * LANES, (i + 1) * LANES)
        gates = ref[...].astype(F32)
        first = jnp.sum(jnp.where(index == rows_ref[0], gates, 0.0), axis=0, keepdims=True)
        second = jnp.sum(jnp.where(index == rows_ref[1], gates, 0.0), axis=0, keepdims=True)
        from_lanes = pl.ds(pl.multiple_of(rows_ref[2 + i] * LANES, LANES), LANES)
        out_ref[:, lanes] = (hidden_ref[:, from_lanes].astype(F32) * first).astype(BF16)
        other_ref[:, lanes] = jnp.broadcast_to(second, (other_ref.shape[0], LANES))


def first_scaled(rows, hidden, packets, extra):
    width, slots = hidden.shape
    tile = width // 2
    last = packets[0].shape[0] // extra - 1
    return pl.pallas_call(
        first_scale_kernel,
        grid_spec=pltpu.PrefetchScalarGridSpec(
            num_scalar_prefetch=1,
            grid=(width // tile,),
            in_specs=[pl.BlockSpec((tile, slots), lambda i, row: (i, 0))]
            + [pl.BlockSpec((extra, LANES), lambda i, row: (last, 0)) for _ in packets],
            out_specs=[
                pl.BlockSpec((tile, slots), lambda i, row: (i, 0)),
                pl.BlockSpec((8, slots), lambda i, row: (0, 0)),
            ],
        ),
        out_shape=[
            jax.ShapeDtypeStruct((width, slots), BF16),
            jax.ShapeDtypeStruct((8, slots), F32),
        ],
        compiler_params=pltpu.CompilerParams(vmem_limit_bytes=VMEM_SCALE),
        cost_estimate=moved(1024),
        name="scale_first",
    )(rows, hidden, *packets)


def second_scale_kernel(gates_ref, *refs):
    for i, ref in enumerate(refs[:-1]):
        lanes = slice(i * LANES, (i + 1) * LANES)
        refs[-1][:, lanes] = (ref[...].astype(F32) * gates_ref[:1, lanes]).astype(BF16)


def second_scaled(gates, packets, out_rows):
    in_specs = [pl.BlockSpec(gates.shape, lambda i: (0, 0))]
    operands = [gates]

    def block_spec(start):
        return pl.BlockSpec((pl.Element(out_rows), pl.Element(LANES)), lambda i: (start, 0))

    for packet, start, count in packets:
        for i in range(count):
            in_specs.append(block_spec(start + i * out_rows))
            operands.append(packet)
    shape = (out_rows, gates.shape[1])
    return pl.pallas_call(
        second_scale_kernel,
        grid=(1,),
        in_specs=in_specs,
        out_specs=pl.BlockSpec(shape, lambda i: (0, 0)),
        out_shape=jax.ShapeDtypeStruct(shape, BF16),
        compiler_params=pltpu.CompilerParams(vmem_limit_bytes=VMEM),
        cost_estimate=moved(1024),
        name="scale_second",
    )(*operands)


def product_kernel(count, add, hidden_ref, *refs):
    tile = refs[0].shape[0]
    rows = jnp.concatenate(
        [
            jnp.concatenate([ref[q:q + LANES, :] for q in range(0, tile, LANES)], axis=1)
            for ref in refs[:count]
        ],
        axis=0,
    )
    product = jnp.dot(hidden_ref[...], rows, preferred_element_type=F32)
    if add:
        product = product + refs[count][...].astype(F32)
    refs[-2][...] = product.astype(refs[-2].dtype)
    refs[-1][...] = jnp.zeros_like(refs[-1])


def block_product(hidden, packets, part, tiles, name, start=0, width=None, add=None, into=None, at=0, size=None, dtype=BF16, vmem=None):
    out_rows = hidden.shape[0]
    size = packets[0].shape[0] if size is None else size
    depth = LANES * len(packets)
    tile_m, tile_n = out_rows // tiles[0], size // tiles[1]

    def out_spec(at):
        return pl.BlockSpec(
            (pl.Element(tile_m), pl.Element(tile_n)),
            lambda j, i: (pl.multiple_of(i * tile_m, 16), pl.multiple_of(at + j * tile_n, LANES)),
        )

    in_specs = [pl.BlockSpec((tile_m, depth), lambda j, i: (i, part))]
    in_specs += [
        pl.BlockSpec(
            (pl.Element(tile_n), pl.Element(LANES)),
            lambda j, i: (pl.multiple_of(start + j * tile_n, 16), 0),
        )
        for _ in packets
    ]
    operands = [hidden, *packets]
    if add is not None:
        in_specs.append(out_spec(0))
        operands.append(add)
    aliases = {}
    if into is not None:
        in_specs.append(pl.BlockSpec(memory_space=pl.ANY))
        aliases = {len(operands): 0}
        operands.append(into)
    return pl.pallas_call(
        functools.partial(product_kernel, len(packets), add is not None),
        grid=(tiles[1], tiles[0]),
        in_specs=in_specs,
        out_specs=[out_spec(at), pl.BlockSpec((8, LANES), lambda j, i: (0, 0))],
        out_shape=[
            jax.ShapeDtypeStruct((out_rows, size if width is None else width), dtype),
            jax.ShapeDtypeStruct((8, LANES), F32),
        ],
        input_output_aliases=aliases,
        compiler_params=pltpu.CompilerParams(vmem_limit_bytes=vmem or VMEM),
        cost_estimate=moved(1024),
        name=name,
    )(*operands)


def gathered(grad_rows, route_ids, bucket_ids, saved_hidden, experts):
    tokens, width = grad_rows.shape[2:]
    steps = experts // 2
    me = lax.axis_index("expert")
    order = jnp.stack(
        [2 * lax.rem(me // 2 + steps - i // 2, steps) + (me % 2 ^ i % 2) for i in range(experts)]
    ).astype(jnp.int32)

    named = route_ids[:, None] == jnp.arange(experts, dtype=jnp.int32)[None, :, None, None]
    gates = (jnp.sum(jnp.where(named, bucket_ids[:, None], 0), axis=3).astype(F32) / 64.0).astype(BF16)
    extra = 2 * experts

    half = width // 2
    cut = round(width * CUT / LANES) * LANES
    span_c, span_d = (0, cut), (cut, width)
    out_rows = saved_hidden.shape[4]

    x, c, d = [None] * steps, [None] * steps, [None] * steps
    x[0], token = pack(grad_rows, 0, [(0, width)], gates.reshape(extra, tokens))
    packet_c, token = pack_second(order, grad_rows, saved_hidden, span_c, range(WITH_C), token)
    packet_d, token = pack_second(order, grad_rows, saved_hidden, span_d, range(WITH_C, experts), token)
    packet_c, packet_d = mirror(packet_c), mirror(packet_d)
    hidden_0, token = turned(saved_hidden, token)
    x[1] = hold(chip_shift(x[0]), token)
    x[2] = chip_shift(x[1])
    c[0] = top(packet_c, span_c[1] - span_c[0], x[C_AFTER])
    c[1] = hold(chip_shift(c[0]), x[2])
    x[3] = chip_shift(x[2])
    c[2] = hold(chip_shift(c[1]), x[3])
    c[3] = chip_shift(c[2])

    def paired(packets):
        return [piece for packet in packets for piece in (packet, core_swap(packet))]

    x = paired(x)
    rows = jnp.concatenate([jnp.stack([me, me + experts]).astype(jnp.int32), order])
    hidden_0, gates_1 = first_scaled(rows, hidden_0, x, extra)
    gates_1 = mirror(gates_1)
    sum_c, token = block_product(
        hidden_0, x, 0, (TM_P, 1), "first_c", 0, size=cut, dtype=SUM, vmem=VMEM_FIRST
    )
    d[0] = top(packet_d, span_d[1] - span_d[0], c[2])
    d[1] = chip_shift(d[0])
    d[1] = hold(d[1], token)
    d[2] = chip_shift(d[1])
    sum_d, token = block_product(
        hidden_0, x, 0, (TM_P, 1), "first_d", cut, size=width - cut, dtype=SUM, vmem=VMEM_FIRST
    )
    d[2] = hold(d[2], token)
    d[3] = chip_shift(d[2])
    hidden_1 = second_scaled(
        gates_1,
        [(packet_c, span_c[1] - span_c[0], WITH_C), (packet_d, span_d[1] - span_d[0], experts - WITH_C)],
        out_rows,
    )
    total, token = block_product(
        hidden_1, paired(c), 0, (2, 2), "second_c", width=width, add=sum_c
    )
    sum_d, token_d = block_product(
        hidden_1, paired(d[:-1]), 0, (2, 1), "second_early_d", add=sum_d, dtype=SUM
    )
    last = hold(d[-1], token, token_d) if HOLD_D else d[-1]
    total, _ = block_product(
        hidden_1, paired([last]), steps - 1, (2, 1), "second_last_d",
        width=width, add=sum_d, into=total, at=cut,
    )
    return total


def on_device(grad_rows, expert_ids, gate_buckets, saved_hidden):
    experts = lax.axis_size("expert")
    capacity = saved_hidden.shape[3] // experts
    tok_count, top_count = expert_ids.shape[2:]
    route_ids, bucket_ids = expert_ids[:, 0], gate_buckets[:, 0]
    if top_count == experts and capacity == tok_count == LANES and experts % 8 == 0:
        result = gathered(grad_rows, route_ids, bucket_ids, saved_hidden, experts)
    else:
        result = routed(
            grad_rows[:, 0], route_ids, bucket_ids, saved_hidden[:, 0, 0], experts, capacity
        )
    return result[None, None]


def solution(mesh):
    return jax.shard_map(
        on_device,
        mesh=mesh,
        in_specs=(
            P(None, "pipe", "expert", None),
            P(None, "pipe", "expert", None),
            P(None, "pipe", "expert", None),
            P(None, "pipe", "expert", None, None),
        ),
        out_specs=P("pipe", "expert", None, None),
        check_vma=False,
    )
```

```python
import functools
import jax
import jax.numpy as jnp
from jax import lax
from jax.experimental import pallas as pl
from jax.experimental.pallas import tpu as pltpu
from jax.sharding import PartitionSpec as P

BF16 = jnp.bfloat16
F32 = jnp.float32
LANES = 128
PARTS = 5
TOKEN = (16, 128)
VMEM_SMALL = 8 << 20
VMEM = 24 << 20
VMEM_PACK = 58 << 20
PINS = {'x1': ['turn'], 'md': ['c0'], 'x2': ['c1'], 'x3': ['c2', 'fc', 'fd'], 'c2': ['x2'], 'c3': ['d1'], 'd0': ['c2'], 'd1': ['lc', 'ld'], 'd3': ['sc', 'ed']}
ORDER = ['x1', 'c1', 'x2', 'c2', 'md', 'd0', 'scale_0', 'first_c', 'first_d', 'x3', 'scale_late', 'late_c', 'late_d', 'd1', 'c3', 'd2', 'scale_1', 'second_c', 'early_d', 'd3']
COSTS = {'x1': 20000000000}
TM_P = 2
VMEM_SCALE = 8 << 20
VMEM_FIRST = 24 << 20
CUT = 0.5715


def mirror(shard):
    ranks = lax.axis_size("pipe")
    return lax.ppermute(shard, "pipe", [(i, ranks - 1 - i) for i in range(ranks)])


def core_swap(shard):
    count = lax.axis_size("expert")
    return lax.ppermute(shard, "expert", [(i, i ^ 1) for i in range(count)])


def chip_shift(shard):
    count = lax.axis_size("expert")
    return lax.ppermute(shard, "expert", [(i, (i + 2) % count) for i in range(count)])


def build_outbound(token_rows, route_ids, bucket_ids, experts, capacity):
    tok_count, top_count = route_ids.shape
    flat_ids = route_ids.reshape(-1)
    one_hot = (flat_ids[:, None] == jnp.arange(experts, dtype=jnp.int32)[None, :]).astype(jnp.int32)
    earlier = jnp.cumsum(one_hot, axis=0) - one_hot
    position = jnp.sum(earlier * one_hot, axis=1)
    slot_ids = flat_ids * capacity + position
    weighting = bucket_ids.reshape(-1).astype(F32) / 64.0
    slot_table = (
        slot_ids[:, None] == jnp.arange(experts * capacity, dtype=jnp.int32)[None, :]
    ).astype(F32)
    slot_table = slot_table * weighting[:, None]
    spread = jnp.sum(slot_table.reshape(tok_count, top_count, experts * capacity), axis=1).astype(BF16)
    outbound = lax.dot_general(
        spread, token_rows, (((0,), (0,)), ((), ())), preferred_element_type=F32
    )
    return outbound.astype(BF16).reshape(experts, capacity, token_rows.shape[1])


def slot_product(hidden_rows, inbound):
    flat_in = inbound.reshape(-1, inbound.shape[-1])
    product = lax.dot_general(
        hidden_rows, flat_in, (((0,), (0,)), ((), ())), preferred_element_type=F32
    )
    return product.astype(BF16)


def routed(token_rows, route_ids, bucket_ids, hidden_rows, experts, capacity):
    partials = []
    for index in range(2):
        outbound = build_outbound(
            token_rows[index], route_ids[index], bucket_ids[index], experts, capacity
        )
        arrived = lax.all_to_all(outbound, "expert", split_axis=0, concat_axis=0, tiled=True)
        partials.append(slot_product(hidden_rows[index], arrived))
    return (partials[0].astype(F32) + mirror(partials[1]).astype(F32)).astype(BF16)


def moved(count):
    return pl.CostEstimate(flops=0, bytes_accessed=1024, transcendentals=0)


def pack_kernel(cut, rows_ref, ids_ref, gates_ref, x_ref, c_ref, token_ref):
    width = rows_ref.shape[3]
    experts = ids_ref.shape[1]
    for start in range(0, width, LANES):
        x_ref[start:start + LANES, :] = rows_ref[0, 0, :, start:start + LANES]
    for start in range(0, cut, LANES):
        c_ref[start:start + LANES, :] = rows_ref[1, 0, :, start:start + LANES]
    named = []
    for direction in range(2):
        ids, gates = ids_ref[direction], gates_ref[direction]
        for expert in range(experts):
            named.append(jnp.sum(jnp.where(ids == expert, gates, 0), axis=0, keepdims=True))
    named = jnp.concatenate(named, axis=0).astype(F32) / 64.0
    x_ref[width:, :] = named.astype(BF16)
    token_ref[...] = jnp.zeros_like(token_ref)


def pack(grad_rows, ids, gates, cut):
    tokens, width = grad_rows.shape[2:]
    shapes = [(width + 2 * ids.shape[1], LANES), (cut, LANES), TOKEN]
    return pl.pallas_call(
        functools.partial(pack_kernel, cut),
        grid=(1,),
        in_specs=[
            pl.BlockSpec(grad_rows.shape, lambda i: (0, 0, 0, 0)),
            pl.BlockSpec(ids.shape, lambda i: (0, 0, 0)),
            pl.BlockSpec(ids.shape, lambda i: (0, 0, 0)),
        ],
        out_specs=[pl.BlockSpec(shape, lambda i: (0, 0)) for shape in shapes],
        out_shape=[jax.ShapeDtypeStruct(shape, BF16) for shape in shapes],
        compiler_params=pltpu.CompilerParams(vmem_limit_bytes=VMEM_PACK),
        cost_estimate=moved(1024),
        name="pack_first",
    )(grad_rows, ids, gates)


def pack_second_kernel(span, order_ref, rows_ref, *refs):
    *hidden_refs, _, out_ref, token_ref = refs
    lo, hi = span
    for start in range(lo, hi, LANES):
        out_ref[start - lo:start - lo + LANES, :] = rows_ref[0, 0, :, start:start + LANES]
    for i, ref in enumerate(hidden_refs):
        base = hi - lo + i * ref.shape[4]
        out_ref[base:base + ref.shape[4], :] = ref[0, 0, 0].T
    token_ref[...] = jnp.zeros_like(token_ref)


def pack_second(order, grad_rows, saved_hidden, span, blocks, dep):
    tokens, width = grad_rows.shape[2:]
    out_rows = saved_hidden.shape[4]
    shape = (span[1] - span[0] + len(blocks) * out_rows, LANES)

    def hidden_spec(i):
        return pl.BlockSpec((1, 1, 1, LANES, out_rows), lambda g, order: (1, 0, 0, order[i], 0))

    return pl.pallas_call(
        functools.partial(pack_second_kernel, span),
        grid_spec=pltpu.PrefetchScalarGridSpec(
            num_scalar_prefetch=1,
            grid=(1,),
            in_specs=[pl.BlockSpec((1, 1, tokens, width), lambda g, order: (1, 0, 0, 0))]
            + [hidden_spec(i) for i in blocks]
            + [pl.BlockSpec(memory_space=pl.ANY)],
            out_specs=[
                pl.BlockSpec(shape, lambda g, order: (0, 0)),
                pl.BlockSpec(TOKEN, lambda g, order: (0, 0)),
            ],
        ),
        out_shape=[jax.ShapeDtypeStruct(shape, BF16), jax.ShapeDtypeStruct(TOKEN, BF16)],
        compiler_params=pltpu.CompilerParams(vmem_limit_bytes=VMEM_PACK),
        cost_estimate=moved(1024),
        name="pack_second",
    )(order, grad_rows, *([saved_hidden] * len(blocks)), dep)


def top_kernel(in_ref, *refs):
    refs[-1][...] = in_ref[...]


def top(value, rows, *deps):
    spec = pl.BlockSpec((rows, LANES), lambda i: (0, 0))
    return pl.pallas_call(
        top_kernel,
        grid=(1,),
        in_specs=[spec] + [pl.BlockSpec(memory_space=pl.ANY)] * len(deps),
        out_specs=spec,
        out_shape=jax.ShapeDtypeStruct((rows, LANES), BF16),
        compiler_params=pltpu.CompilerParams(vmem_limit_bytes=VMEM_SMALL),
        cost_estimate=moved(1024),
        name="top_rows",
    )(value, *deps)


def hold_kernel(*refs):
    pass


def hold(value, *deps, flops=0):
    return pl.pallas_call(
        hold_kernel,
        in_specs=[pl.BlockSpec(memory_space=pl.ANY)] * (1 + len(deps)),
        out_specs=pl.BlockSpec(memory_space=pl.ANY),
        out_shape=jax.ShapeDtypeStruct(value.shape, value.dtype),
        input_output_aliases={0: 0},
        compiler_params=pltpu.CompilerParams(vmem_limit_bytes=VMEM_SMALL),
        cost_estimate=pl.CostEstimate(flops=flops, bytes_accessed=1024, transcendentals=0),
        name="hold",
    )(value, *deps)


def turn_kernel(hidden_ref, _, out_ref, token_ref):
    slots = hidden_ref.shape[3]
    for i in range(slots // LANES):
        lanes = slice(i * LANES, (i + 1) * LANES)
        out_ref[:, lanes] = hidden_ref[0, 0, 0, lanes, :].T
    token_ref[...] = jnp.zeros_like(token_ref)


def turned(saved_hidden, dep):
    slots, width = saved_hidden.shape[3:]
    return pl.pallas_call(
        turn_kernel,
        grid=(1,),
        in_specs=[
            pl.BlockSpec((1, 1, 1, slots, width), lambda i: (0, 0, 0, 0, 0)),
            pl.BlockSpec(memory_space=pl.ANY),
        ],
        out_specs=[
            pl.BlockSpec((width, slots), lambda i: (0, 0)),
            pl.BlockSpec(TOKEN, lambda i: (0, 0)),
        ],
        out_shape=[jax.ShapeDtypeStruct((width, slots), BF16), jax.ShapeDtypeStruct(TOKEN, BF16)],
        compiler_params=pltpu.CompilerParams(vmem_limit_bytes=VMEM_PACK),
        cost_estimate=moved(1024),
        name="turn_hidden",
    )(saved_hidden, dep)


def first_scale_kernel(rows_ref, hidden_ref, *refs):
    *packet_refs, out_ref, other_ref = refs
    index = lax.broadcasted_iota(jnp.int32, packet_refs[0].shape, 0)
    for i, ref in enumerate(packet_refs):
        lanes = slice(i * LANES, (i + 1) * LANES)
        gates = ref[...].astype(F32)
        first = jnp.sum(jnp.where(index == rows_ref[0], gates, 0.0), axis=0, keepdims=True)
        second = jnp.sum(jnp.where(index == rows_ref[1], gates, 0.0), axis=0, keepdims=True)
        from_lanes = pl.ds(pl.multiple_of(rows_ref[2 + i] * LANES, LANES), LANES)
        out_ref[:, lanes] = (hidden_ref[:, from_lanes].astype(F32) * first).astype(BF16)
        other_ref[:, lanes] = jnp.broadcast_to(second, (other_ref.shape[0], LANES))


def first_scaled(rows, hidden, packets, extra):
    width, slots = hidden.shape
    depth = LANES * len(packets)
    tile = width // 2
    last = packets[0].shape[0] // extra - 1
    return pl.pallas_call(
        first_scale_kernel,
        grid_spec=pltpu.PrefetchScalarGridSpec(
            num_scalar_prefetch=1,
            grid=(width // tile,),
            in_specs=[pl.BlockSpec((tile, slots), lambda i, row: (i, 0))]
            + [pl.BlockSpec((extra, LANES), lambda i, row: (last, 0)) for _ in packets],
            out_specs=[
                pl.BlockSpec((tile, depth), lambda i, row: (i, 0)),
                pl.BlockSpec((8, depth), lambda i, row: (0, 0)),
            ],
        ),
        out_shape=[
            jax.ShapeDtypeStruct((width, depth), BF16),
            jax.ShapeDtypeStruct((8, depth), F32),
        ],
        compiler_params=pltpu.CompilerParams(vmem_limit_bytes=VMEM_SCALE),
        cost_estimate=moved(1024),
        name="scale_first",
    )(rows, hidden, *packets)


def second_scale_kernel(early_ref, late_ref, *refs):
    early = early_ref.shape[1]
    out_ref, token_ref = refs[-2:]
    token_ref[...] = jnp.zeros_like(token_ref)
    for i, ref in enumerate(refs[:-2]):
        lanes = slice(i * LANES, (i + 1) * LANES)
        if i * LANES < early:
            gates = early_ref[:1, lanes]
        else:
            gates = late_ref[:1, i * LANES - early:(i + 1) * LANES - early]
        out_ref[:, lanes] = (ref[...].astype(F32) * gates).astype(BF16)


def second_scaled(early, late, packet, start, out_rows):
    slots = early.shape[1] + late.shape[1]

    def block_spec(row):
        return pl.BlockSpec((pl.Element(out_rows), pl.Element(LANES)), lambda i: (row, 0))

    blocks = [block_spec(start + i * out_rows) for i in range(slots // LANES)]
    return pl.pallas_call(
        second_scale_kernel,
        grid=(1,),
        in_specs=[
            pl.BlockSpec(early.shape, lambda i: (0, 0)),
            pl.BlockSpec(late.shape, lambda i: (0, 0)),
        ]
        + blocks,
        out_specs=[
            pl.BlockSpec((out_rows, slots), lambda i: (0, 0)),
            pl.BlockSpec(TOKEN, lambda i: (0, 0)),
        ],
        out_shape=[jax.ShapeDtypeStruct((out_rows, slots), BF16), jax.ShapeDtypeStruct(TOKEN, BF16)],
        compiler_params=pltpu.CompilerParams(vmem_limit_bytes=VMEM),
        cost_estimate=moved(1024),
        name="scale_second",
    )(early, late, *([packet] * len(blocks)))


def product_kernel(count, add, hidden_ref, *refs):
    tile = refs[0].shape[0]
    rows = jnp.concatenate(
        [
            jnp.concatenate([ref[q:q + LANES, :] for q in range(0, tile, LANES)], axis=1)
            for ref in refs[:count]
        ],
        axis=0,
    )
    product = jnp.dot(hidden_ref[...], rows, preferred_element_type=F32)
    if add:
        product = product + refs[count][...].astype(F32)
    refs[-2][...] = product.astype(refs[-2].dtype)
    refs[-1][...] = jnp.zeros_like(refs[-1])


def block_product(hidden, packets, part, tiles, name, start=0, width=None, add=None, into=None, at=0, size=None, dtype=BF16, vmem=None):
    out_rows = hidden.shape[0]
    size = packets[0].shape[0] if size is None else size
    depth = LANES * len(packets)
    tile_m, tile_n = out_rows // tiles[0], size // tiles[1]

    def out_spec(at):
        return pl.BlockSpec(
            (pl.Element(tile_m), pl.Element(tile_n)),
            lambda j, i: (pl.multiple_of(i * tile_m, 16), pl.multiple_of(at + j * tile_n, LANES)),
        )

    in_specs = [pl.BlockSpec((tile_m, depth), lambda j, i: (i, part))]
    in_specs += [
        pl.BlockSpec(
            (pl.Element(tile_n), pl.Element(LANES)),
            lambda j, i: (pl.multiple_of(start + j * tile_n, 16), 0),
        )
        for _ in packets
    ]
    operands = [hidden, *packets]
    if add is not None:
        in_specs.append(out_spec(0))
        operands.append(add)
    aliases = {}
    if into is not None:
        in_specs.append(pl.BlockSpec(memory_space=pl.ANY))
        aliases = {len(operands): 0}
        operands.append(into)
    return pl.pallas_call(
        functools.partial(product_kernel, len(packets), add is not None),
        grid=(tiles[1], tiles[0]),
        in_specs=in_specs,
        out_specs=[out_spec(at), pl.BlockSpec((8, LANES), lambda j, i: (0, 0))],
        out_shape=[
            jax.ShapeDtypeStruct((out_rows, size if width is None else width), dtype),
            jax.ShapeDtypeStruct((8, LANES), F32),
        ],
        input_output_aliases=aliases,
        compiler_params=pltpu.CompilerParams(vmem_limit_bytes=vmem or VMEM),
        cost_estimate=moved(1024),
        name=name,
    )(*operands)


def gathered(grad_rows, route_ids, bucket_ids, saved_hidden, experts):
    tokens, width = grad_rows.shape[2:]
    steps = experts // 2
    me = lax.axis_index("expert")
    order = jnp.stack(
        [2 * lax.rem(me // 2 + steps - i // 2, steps) + (me % 2 ^ i % 2) for i in range(experts)]
    ).astype(jnp.int32)

    extra = 2 * experts

    cut = round(width * CUT / LANES) * LANES
    span_c, span_d = (0, cut), (cut, width)
    out_rows = saved_hidden.shape[4]

    done = {}

    def pinned(name, value):
        deps = [done[dep] for dep in PINS.get(name, ())]
        return hold(value, *deps, flops=COSTS.get(name, 0)) if deps else value

    def note(name, value):
        done[name] = value
        return value

    x, c, d = [None] * steps, [None] * steps, [None] * steps
    ids, buckets = jnp.swapaxes(route_ids, 1, 2), jnp.swapaxes(bucket_ids, 1, 2)
    x[0], packet_c, token = pack(grad_rows, ids, buckets, cut)
    packet_d, token = pack_second(order, grad_rows, saved_hidden, span_d, range(experts), token)
    c[0] = note("c0", mirror(packet_c))
    hidden_0, token = turned(saved_hidden, token)
    note("turn", token)

    def paired(packets):
        return [piece for packet in packets for piece in (packet, core_swap(packet))]

    results = {}

    def move(name):
        packets, step = dict(x=x, c=c, d=d)[name[0]], int(name[1])
        if step:
            packets[step] = note(name, pinned(name, chip_shift(packets[step - 1])))
        else:
            pins = [done[dep] for dep in PINS.get(name, ())]
            packets[0] = note(name, top(results["md"], width - cut, *pins))

    def mirror_d():
        results["md"] = mirror(pinned("md", packet_d))

    def scale_0():
        picked = jnp.concatenate([jnp.stack([me, me + experts]).astype(jnp.int32), order[:early]])
        results["x"] = paired(x[:-1])
        results["h0"], gates = first_scaled(picked, hidden_0, results["x"], extra)
        results["g"] = mirror(gates)

    def first_c():
        results["c"], token = block_product(
            results["h0"], results["x"], 0, (TM_P, 1), "first_c", 0, size=cut, vmem=VMEM_FIRST
        )
        note("fc", token)

    def first_d():
        results["d"], token = block_product(
            results["h0"], results["x"], 0, (TM_P, 1), "first_d", cut, size=width - cut, vmem=VMEM_FIRST
        )
        note("fd", token)

    def scale_late():
        picked = jnp.concatenate([jnp.stack([me, me + experts]).astype(jnp.int32), order[early:]])
        results["xl"] = paired(x[-1:])
        results["hl"], gates = first_scaled(picked, hidden_0, results["xl"], extra)
        results["gl"] = mirror(gates)

    def late_c():
        results["c"], token = block_product(
            results["hl"], results["xl"], 0, (2, 1), "late_c", 0, size=cut, add=results["c"]
        )
        note("lc", token)

    def late_d():
        results["d"], token = block_product(
            results["hl"], results["xl"], 0, (2, 1), "late_d", cut, size=width - cut, add=results["d"]
        )
        note("ld", token)

    def scale_1():
        results["h1"], token = second_scaled(
            results["g"], results["gl"], results["md"], width - cut, out_rows
        )
        note("s1", token)

    def second_c():
        results["total"], token = block_product(
            results["h1"], paired(c), 0, (2, 2), "second_c", width=width, add=results["c"]
        )
        note("sc", token)

    def early_d():
        results["d"], token = block_product(
            results["h1"], paired(d[:-1]), 0, (2, 1), "second_early_d", add=results["d"]
        )
        note("ed", token)

    early = 2 * (steps - 1)
    kernels = dict(
        md=mirror_d, scale_0=scale_0, first_c=first_c, first_d=first_d, scale_late=scale_late, late_c=late_c,
        late_d=late_d, scale_1=scale_1, second_c=second_c, early_d=early_d,
    )
    for name in ORDER:
        if name in kernels:
            kernels[name]()
        else:
            move(name)
    total, _ = block_product(
        results["h1"], paired([d[-1]]), steps - 1, (2, 1), "second_last_d",
        width=width, add=results["d"], into=results["total"], at=cut,
    )
    return total


def on_device(grad_rows, expert_ids, gate_buckets, saved_hidden):
    experts = lax.axis_size("expert")
    capacity = saved_hidden.shape[3] // experts
    tok_count, top_count = expert_ids.shape[2:]
    route_ids, bucket_ids = expert_ids[:, 0], gate_buckets[:, 0]
    if top_count == experts and capacity == tok_count == LANES and experts % 8 == 0:
        result = gathered(grad_rows, route_ids, bucket_ids, saved_hidden, experts)
    else:
        result = routed(
            grad_rows[:, 0], route_ids, bucket_ids, saved_hidden[:, 0, 0], experts, capacity
        )
    return result[None, None]


def solution(mesh):
    return jax.shard_map(
        on_device,
        mesh=mesh,
        in_specs=(
            P(None, "pipe", "expert", None),
            P(None, "pipe", "expert", None),
            P(None, "pipe", "expert", None),
            P(None, "pipe", "expert", None, None),
        ),
        out_specs=P("pipe", "expert", None, None),
        check_vma=False,
    )
```

```python
import functools
import jax
import jax.numpy as jnp
from jax import lax
from jax.experimental import pallas as pl
from jax.experimental.pallas import tpu as pltpu
from jax.sharding import PartitionSpec as P

BF16 = jnp.bfloat16
F32 = jnp.float32
LANES = 128
TOKEN = (16, 128)
VMEM_SMALL = 8 << 20
VMEM = 24 << 20
VMEM_PACK = 58 << 20
PINS = {'x1': ['turn'], 'md': ['c0'], 'x2': ['c1'], 'x3': ['c2', 'fc', 'fd'], 'c2': ['x2'], 'c3': ['d1'], 'd0': ['c2'], 'd1': ['lc', 'ld'], 'd3': ['sc', 'ed']}
ORDER = ['x1', 'c1', 'x2', 'c2', 'md', 'd0', 'scale_0', 'first_c', 'first_d', 'x3', 'scale_late', 'late_c', 'late_d', 'd1', 'c3', 'd2', 'scale_1', 'second_c', 'early_d', 'd3']
COSTS = {'x1': 20000000000}
WORK = {}
TM_P = 5
TILES_C = (2, 2)
TILES_L = (2, 1)
VMEM_SCALE = 8 << 20
VMEM_FIRST = 24 << 20
CUT = 0.5715


def mirror(shard):
    ranks = lax.axis_size("pipe")
    return lax.ppermute(shard, "pipe", [(i, ranks - 1 - i) for i in range(ranks)])


def core_swap(shard):
    count = lax.axis_size("expert")
    return lax.ppermute(shard, "expert", [(i, i ^ 1) for i in range(count)])


def chip_shift(shard):
    count = lax.axis_size("expert")
    return lax.ppermute(shard, "expert", [(i, (i + 2) % count) for i in range(count)])


def build_outbound(token_rows, route_ids, bucket_ids, experts, capacity):
    tok_count, top_count = route_ids.shape
    flat_ids = route_ids.reshape(-1)
    one_hot = (flat_ids[:, None] == jnp.arange(experts, dtype=jnp.int32)[None, :]).astype(jnp.int32)
    earlier = jnp.cumsum(one_hot, axis=0) - one_hot
    position = jnp.sum(earlier * one_hot, axis=1)
    slot_ids = flat_ids * capacity + position
    weighting = bucket_ids.reshape(-1).astype(F32) / 64.0
    slot_table = (
        slot_ids[:, None] == jnp.arange(experts * capacity, dtype=jnp.int32)[None, :]
    ).astype(F32)
    slot_table = slot_table * weighting[:, None]
    spread = jnp.sum(slot_table.reshape(tok_count, top_count, experts * capacity), axis=1).astype(BF16)
    outbound = lax.dot_general(
        spread, token_rows, (((0,), (0,)), ((), ())), preferred_element_type=F32
    )
    return outbound.astype(BF16).reshape(experts, capacity, token_rows.shape[1])


def slot_product(hidden_rows, inbound):
    flat_in = inbound.reshape(-1, inbound.shape[-1])
    product = lax.dot_general(
        hidden_rows, flat_in, (((0,), (0,)), ((), ())), preferred_element_type=F32
    )
    return product.astype(BF16)


def routed(token_rows, route_ids, bucket_ids, hidden_rows, experts, capacity):
    partials = []
    for index in range(2):
        outbound = build_outbound(
            token_rows[index], route_ids[index], bucket_ids[index], experts, capacity
        )
        arrived = lax.all_to_all(outbound, "expert", split_axis=0, concat_axis=0, tiled=True)
        partials.append(slot_product(hidden_rows[index], arrived))
    return (partials[0].astype(F32) + mirror(partials[1]).astype(F32)).astype(BF16)


def moved(count):
    return pl.CostEstimate(flops=0, bytes_accessed=1024, transcendentals=0)


def pack_kernel(cut, rows_ref, ids_ref, gates_ref, x_ref, c_ref, token_ref):
    width = rows_ref.shape[3]
    experts = ids_ref.shape[1]
    for start in range(0, width, LANES):
        x_ref[start:start + LANES, :] = rows_ref[0, 0, :, start:start + LANES]
    for start in range(0, cut, LANES):
        c_ref[start:start + LANES, :] = rows_ref[1, 0, :, start:start + LANES]
    named = []
    for direction in range(2):
        ids, gates = ids_ref[direction], gates_ref[direction]
        for expert in range(experts):
            named.append(jnp.sum(jnp.where(ids == expert, gates, 0), axis=0, keepdims=True))
    named = jnp.concatenate(named, axis=0).astype(F32) / 64.0
    x_ref[width:, :] = named.astype(BF16)
    token_ref[...] = jnp.zeros_like(token_ref)


def pack(grad_rows, ids, gates, cut):
    tokens, width = grad_rows.shape[2:]
    shapes = [(width + 2 * ids.shape[1], LANES), (cut, LANES), TOKEN]
    return pl.pallas_call(
        functools.partial(pack_kernel, cut),
        grid=(1,),
        in_specs=[
            pl.BlockSpec(grad_rows.shape, lambda i: (0, 0, 0, 0)),
            pl.BlockSpec(ids.shape, lambda i: (0, 0, 0)),
            pl.BlockSpec(ids.shape, lambda i: (0, 0, 0)),
        ],
        out_specs=[pl.BlockSpec(shape, lambda i: (0, 0)) for shape in shapes],
        out_shape=[jax.ShapeDtypeStruct(shape, BF16) for shape in shapes],
        compiler_params=pltpu.CompilerParams(vmem_limit_bytes=VMEM_PACK),
        cost_estimate=moved(1024),
        name="pack_first",
    )(grad_rows, ids, gates)


def pack_second_kernel(span, order_ref, rows_ref, *refs):
    *hidden_refs, _, out_ref, token_ref = refs
    lo, hi = span
    for start in range(lo, hi, LANES):
        out_ref[start - lo:start - lo + LANES, :] = rows_ref[0, 0, :, start:start + LANES]
    for i, ref in enumerate(hidden_refs):
        base = hi - lo + i * ref.shape[4]
        out_ref[base:base + ref.shape[4], :] = ref[0, 0, 0].T
    token_ref[...] = jnp.zeros_like(token_ref)


def pack_second(order, grad_rows, saved_hidden, span, blocks, dep):
    tokens, width = grad_rows.shape[2:]
    out_rows = saved_hidden.shape[4]
    shape = (span[1] - span[0] + len(blocks) * out_rows, LANES)

    def hidden_spec(i):
        return pl.BlockSpec((1, 1, 1, LANES, out_rows), lambda g, order: (1, 0, 0, order[i], 0))

    return pl.pallas_call(
        functools.partial(pack_second_kernel, span),
        grid_spec=pltpu.PrefetchScalarGridSpec(
            num_scalar_prefetch=1,
            grid=(1,),
            in_specs=[pl.BlockSpec((1, 1, tokens, width), lambda g, order: (1, 0, 0, 0))]
            + [hidden_spec(i) for i in blocks]
            + [pl.BlockSpec(memory_space=pl.ANY)],
            out_specs=[
                pl.BlockSpec(shape, lambda g, order: (0, 0)),
                pl.BlockSpec(TOKEN, lambda g, order: (0, 0)),
            ],
        ),
        out_shape=[jax.ShapeDtypeStruct(shape, BF16), jax.ShapeDtypeStruct(TOKEN, BF16)],
        compiler_params=pltpu.CompilerParams(vmem_limit_bytes=VMEM_PACK),
        cost_estimate=moved(1024),
        name="pack_second",
    )(order, grad_rows, *([saved_hidden] * len(blocks)), dep)


def top_kernel(in_ref, *refs):
    refs[-1][...] = in_ref[...]


def top(value, rows, *deps):
    spec = pl.BlockSpec((rows, LANES), lambda i: (0, 0))
    return pl.pallas_call(
        top_kernel,
        grid=(1,),
        in_specs=[spec] + [pl.BlockSpec(memory_space=pl.ANY)] * len(deps),
        out_specs=spec,
        out_shape=jax.ShapeDtypeStruct((rows, LANES), BF16),
        compiler_params=pltpu.CompilerParams(vmem_limit_bytes=VMEM_SMALL),
        cost_estimate=moved(1024),
        name="top_rows",
    )(value, *deps)


def hold_kernel(*refs):
    pass


def hold(value, *deps, flops=0):
    return pl.pallas_call(
        hold_kernel,
        in_specs=[pl.BlockSpec(memory_space=pl.ANY)] * (1 + len(deps)),
        out_specs=pl.BlockSpec(memory_space=pl.ANY),
        out_shape=jax.ShapeDtypeStruct(value.shape, value.dtype),
        input_output_aliases={0: 0},
        compiler_params=pltpu.CompilerParams(vmem_limit_bytes=VMEM_SMALL),
        cost_estimate=pl.CostEstimate(flops=flops, bytes_accessed=1024, transcendentals=0),
        name="hold",
    )(value, *deps)


def turn_kernel(hidden_ref, _, out_ref, token_ref):
    slots = hidden_ref.shape[3]
    for i in range(slots // LANES):
        lanes = slice(i * LANES, (i + 1) * LANES)
        out_ref[:, lanes] = hidden_ref[0, 0, 0, lanes, :].T
    token_ref[...] = jnp.zeros_like(token_ref)


def turned(saved_hidden, dep):
    slots, width = saved_hidden.shape[3:]
    return pl.pallas_call(
        turn_kernel,
        grid=(1,),
        in_specs=[
            pl.BlockSpec((1, 1, 1, slots, width), lambda i: (0, 0, 0, 0, 0)),
            pl.BlockSpec(memory_space=pl.ANY),
        ],
        out_specs=[
            pl.BlockSpec((width, slots), lambda i: (0, 0)),
            pl.BlockSpec(TOKEN, lambda i: (0, 0)),
        ],
        out_shape=[jax.ShapeDtypeStruct((width, slots), BF16), jax.ShapeDtypeStruct(TOKEN, BF16)],
        compiler_params=pltpu.CompilerParams(vmem_limit_bytes=VMEM_PACK),
        cost_estimate=moved(1024),
        name="turn_hidden",
    )(saved_hidden, dep)


def first_scale_kernel(rows_ref, hidden_ref, *refs):
    *packet_refs, out_ref, other_ref = refs
    index = lax.broadcasted_iota(jnp.int32, packet_refs[0].shape, 0)
    for i, ref in enumerate(packet_refs):
        lanes = slice(i * LANES, (i + 1) * LANES)
        gates = ref[...].astype(F32)
        first = jnp.sum(jnp.where(index == rows_ref[0], gates, 0.0), axis=0, keepdims=True)
        second = jnp.sum(jnp.where(index == rows_ref[1], gates, 0.0), axis=0, keepdims=True)
        from_lanes = pl.ds(pl.multiple_of(rows_ref[2 + i] * LANES, LANES), LANES)
        out_ref[:, lanes] = (hidden_ref[:, from_lanes].astype(F32) * first).astype(BF16)
        other_ref[:, lanes] = jnp.broadcast_to(second, (other_ref.shape[0], LANES))


def first_scaled(rows, hidden, packets, extra):
    width, slots = hidden.shape
    depth = LANES * len(packets)
    tile = width // 2
    last = packets[0].shape[0] // extra - 1
    return pl.pallas_call(
        first_scale_kernel,
        grid_spec=pltpu.PrefetchScalarGridSpec(
            num_scalar_prefetch=1,
            grid=(width // tile,),
            in_specs=[pl.BlockSpec((tile, slots), lambda i, row: (i, 0))]
            + [pl.BlockSpec((extra, LANES), lambda i, row: (last, 0)) for _ in packets],
            out_specs=[
                pl.BlockSpec((tile, depth), lambda i, row: (i, 0)),
                pl.BlockSpec((8, depth), lambda i, row: (0, 0)),
            ],
        ),
        out_shape=[
            jax.ShapeDtypeStruct((width, depth), BF16),
            jax.ShapeDtypeStruct((8, depth), F32),
        ],
        compiler_params=pltpu.CompilerParams(vmem_limit_bytes=VMEM_SCALE),
        cost_estimate=moved(1024),
        name="scale_first",
    )(rows, hidden, *packets)


def second_scale_kernel(early_ref, late_ref, *refs):
    early = early_ref.shape[1]
    out_ref, token_ref = refs[-2:]
    token_ref[...] = jnp.zeros_like(token_ref)
    for i, ref in enumerate(refs[:-2]):
        lanes = slice(i * LANES, (i + 1) * LANES)
        if i * LANES < early:
            gates = early_ref[:1, lanes]
        else:
            gates = late_ref[:1, i * LANES - early:(i + 1) * LANES - early]
        out_ref[:, lanes] = (ref[...].astype(F32) * gates).astype(BF16)


def second_scaled(early, late, packet, start, out_rows):
    slots = early.shape[1] + late.shape[1]

    def block_spec(row):
        return pl.BlockSpec((pl.Element(out_rows), pl.Element(LANES)), lambda i: (row, 0))

    blocks = [block_spec(start + i * out_rows) for i in range(slots // LANES)]
    return pl.pallas_call(
        second_scale_kernel,
        grid=(1,),
        in_specs=[
            pl.BlockSpec(early.shape, lambda i: (0, 0)),
            pl.BlockSpec(late.shape, lambda i: (0, 0)),
        ]
        + blocks,
        out_specs=[
            pl.BlockSpec((out_rows, slots), lambda i: (0, 0)),
            pl.BlockSpec(TOKEN, lambda i: (0, 0)),
        ],
        out_shape=[jax.ShapeDtypeStruct((out_rows, slots), BF16), jax.ShapeDtypeStruct(TOKEN, BF16)],
        compiler_params=pltpu.CompilerParams(vmem_limit_bytes=VMEM),
        cost_estimate=moved(1024),
        name="scale_second",
    )(early, late, *([packet] * len(blocks)))


def product_kernel(count, add, hidden_ref, *refs):
    tile = refs[0].shape[0]
    rows = jnp.concatenate(
        [
            jnp.concatenate([ref[q:q + LANES, :] for q in range(0, tile, LANES)], axis=1)
            for ref in refs[:count]
        ],
        axis=0,
    )
    product = jnp.dot(hidden_ref[...], rows, preferred_element_type=F32)
    if add:
        product = product + refs[count][...].astype(F32)
    refs[-2][...] = product.astype(refs[-2].dtype)
    refs[-1][...] = jnp.zeros_like(refs[-1])


def block_product(hidden, packets, part, tiles, name, start=0, width=None, add=None, into=None, at=0, size=None, dtype=BF16, vmem=None):
    out_rows = hidden.shape[0]
    size = packets[0].shape[0] if size is None else size
    depth = LANES * len(packets)
    tile_m, tile_n = out_rows // tiles[0], size // tiles[1]

    def out_spec(at):
        return pl.BlockSpec(
            (pl.Element(tile_m), pl.Element(tile_n)),
            lambda j, i: (pl.multiple_of(i * tile_m, 16), pl.multiple_of(at + j * tile_n, LANES)),
        )

    in_specs = [pl.BlockSpec((tile_m, depth), lambda j, i: (i, part))]
    in_specs += [
        pl.BlockSpec(
            (pl.Element(tile_n), pl.Element(LANES)),
            lambda j, i: (pl.multiple_of(start + j * tile_n, 16), 0),
        )
        for _ in packets
    ]
    operands = [hidden, *packets]
    if add is not None:
        in_specs.append(out_spec(0))
        operands.append(add)
    aliases = {}
    if into is not None:
        in_specs.append(pl.BlockSpec(memory_space=pl.ANY))
        aliases = {len(operands): 0}
        operands.append(into)
    return pl.pallas_call(
        functools.partial(product_kernel, len(packets), add is not None),
        grid=(tiles[1], tiles[0]),
        in_specs=in_specs,
        out_specs=[out_spec(at), pl.BlockSpec((8, LANES), lambda j, i: (0, 0))],
        out_shape=[
            jax.ShapeDtypeStruct((out_rows, size if width is None else width), dtype),
            jax.ShapeDtypeStruct((8, LANES), F32),
        ],
        input_output_aliases=aliases,
        compiler_params=pltpu.CompilerParams(vmem_limit_bytes=vmem or VMEM),
        cost_estimate=pl.CostEstimate(flops=WORK.get(name, 0), bytes_accessed=1024, transcendentals=0),
        name=name,
    )(*operands)


def gathered(grad_rows, route_ids, bucket_ids, saved_hidden, experts):
    tokens, width = grad_rows.shape[2:]
    steps = experts // 2
    me = lax.axis_index("expert")
    order = jnp.stack(
        [2 * lax.rem(me // 2 + steps - i // 2, steps) + (me % 2 ^ i % 2) for i in range(experts)]
    ).astype(jnp.int32)

    extra = 2 * experts

    cut = round(width * CUT / LANES) * LANES
    span_c, span_d = (0, cut), (cut, width)
    out_rows = saved_hidden.shape[4]

    done = {}

    def pinned(name, value):
        deps = [done[dep] for dep in PINS.get(name, ())]
        return hold(value, *deps, flops=COSTS.get(name, 0)) if deps else value

    def note(name, value):
        done[name] = value
        return value

    x, c, d = [None] * steps, [None] * steps, [None] * steps
    ids, buckets = jnp.swapaxes(route_ids, 1, 2), jnp.swapaxes(bucket_ids, 1, 2)
    x[0], packet_c, token = pack(grad_rows, ids, buckets, cut)
    packet_d, token = pack_second(order, grad_rows, saved_hidden, span_d, range(experts), token)
    c[0] = note("c0", mirror(packet_c))
    hidden_0, token = turned(saved_hidden, token)
    note("turn", token)

    def paired(packets):
        return [piece for packet in packets for piece in (packet, core_swap(packet))]

    results = {}

    def move(name):
        packets, step = dict(x=x, c=c, d=d)[name[0]], int(name[1])
        if step:
            packets[step] = note(name, pinned(name, chip_shift(packets[step - 1])))
        else:
            pins = [done[dep] for dep in PINS.get(name, ())]
            packets[0] = note(name, top(results["md"], width - cut, *pins))

    def mirror_d():
        results["md"] = mirror(pinned("md", packet_d))

    def scale_0():
        picked = jnp.concatenate([jnp.stack([me, me + experts]).astype(jnp.int32), order[:early]])
        results["x"] = paired(x[:-1])
        results["h0"], gates = first_scaled(picked, hidden_0, results["x"], extra)
        results["g"] = mirror(gates)

    def first_c():
        results["c"], token = block_product(
            results["h0"], results["x"], 0, (TM_P, 1), "first_c", 0, size=cut, vmem=VMEM_FIRST
        )
        note("fc", token)

    def first_d():
        results["d"], token = block_product(
            results["h0"], results["x"], 0, (TM_P, 1), "first_d", cut, size=width - cut, vmem=VMEM_FIRST
        )
        note("fd", token)

    def scale_late():
        picked = jnp.concatenate([jnp.stack([me, me + experts]).astype(jnp.int32), order[early:]])
        results["xl"] = paired(x[-1:])
        results["hl"], gates = first_scaled(picked, hidden_0, results["xl"], extra)
        results["gl"] = mirror(gates)

    def late_c():
        results["c"], token = block_product(
            results["hl"], results["xl"], 0, (2, 1), "late_c", 0, size=cut, add=results["c"]
        )
        note("lc", token)

    def late_d():
        results["d"], token = block_product(
            results["hl"], results["xl"], 0, (2, 1), "late_d", cut, size=width - cut, add=results["d"]
        )
        note("ld", token)

    def scale_1():
        results["h1"], token = second_scaled(
            results["g"], results["gl"], results["md"], width - cut, out_rows
        )
        note("s1", token)

    def second_c():
        results["total"], token = block_product(
            results["h1"], paired(c), 0, TILES_C, "second_c", width=width, add=results["c"]
        )
        note("sc", token)

    def early_d():
        results["d"], token = block_product(
            results["h1"], paired(d[:-1]), 0, (2, 1), "second_early_d", add=results["d"]
        )
        note("ed", token)

    early = 2 * (steps - 1)
    kernels = dict(
        md=mirror_d, scale_0=scale_0, first_c=first_c, first_d=first_d, scale_late=scale_late, late_c=late_c,
        late_d=late_d, scale_1=scale_1, second_c=second_c, early_d=early_d,
    )
    for name in ORDER:
        if name in kernels:
            kernels[name]()
        else:
            move(name)
    total, _ = block_product(
        results["h1"], paired([d[-1]]), steps - 1, TILES_L, "second_last_d",
        width=width, add=results["d"], into=results["total"], at=cut,
    )
    return total


def on_device(grad_rows, expert_ids, gate_buckets, saved_hidden):
    experts = lax.axis_size("expert")
    capacity = saved_hidden.shape[3] // experts
    tok_count, top_count = expert_ids.shape[2:]
    route_ids, bucket_ids = expert_ids[:, 0], gate_buckets[:, 0]
    if top_count == experts and capacity == tok_count == LANES and experts % 8 == 0:
        result = gathered(grad_rows, route_ids, bucket_ids, saved_hidden, experts)
    else:
        result = routed(
            grad_rows[:, 0], route_ids, bucket_ids, saved_hidden[:, 0, 0], experts, capacity
        )
    return result[None, None]


def solution(mesh):
    return jax.shard_map(
        on_device,
        mesh=mesh,
        in_specs=(
            P(None, "pipe", "expert", None),
            P(None, "pipe", "expert", None),
            P(None, "pipe", "expert", None),
            P(None, "pipe", "expert", None, None),
        ),
        out_specs=P("pipe", "expert", None, None),
        check_vma=False,
    )
```
